128 devices in a mesh: tm: 16 (over y_hi, z, core), space: 8 (over x, y_lo).
Axes of the slice: x: 4, y: 4 (y_hi: 2, y_lo: 2; y = y_hi * 2 + y_lo), z: 4, core: 2. Of those that a mesh axis runs over, the one named last changes fastest.
Arguments:
- query: bfloat16 [32, 2048, 3072], P('tm', 'space'), may hold values from -204 to 204
- key_proj: bfloat16 [32, 2048, 3072], P('tm', 'space'), may hold values from -6 to 6
- value: bfloat16 [32, 2048, 3072], P('tm', 'space'), may hold values from -6 to 6
- head_class: int32 [24], replicated, may hold values from 0 to 1, as said below
- frame_count: int32 [1], replicated, may hold values from 24 to 31
Outputs:
- attended: bfloat16 [32, 2048, 3072], P('tm', 'space')
The draws below stay inside these ranges and needn't reach their ends.
Inputs may be any that keep to these rules, and one draw needn't show every extreme that they name: `head_class`: exactly 8 of the 24 heads are temporal, the others spatial. Frames of index frame_count[0] or more are padding.
All inputs are finite; a program needn't handle non-finite values.
Results may differ from the reference program's by a relative error of at most 0.0085.
Values may be sent and summed in bfloat16 or wider, within the bound.
A program may use at most 320 MiB of HBM per device.

```python
import jax
import jax.numpy as jnp
from jax import lax

HEADS = 24
HD = 128
TEMP_HEADS = 8
FR_DEV = 2
FRAMES = 32
POS = 2048


def shared_rows(key):
    return jnp.clip(jax.random.normal(key, (FRAMES, POS, HEADS * HD), jnp.float32), -6.0, 6.0)


def draw_key_proj(key, part):
    shared_base = shared_rows(key)
    return shared_base.astype(jnp.bfloat16)


def draw_query(key, part):
    key = jax.random.fold_in(key, 12)
    own_rows = jnp.clip(jax.random.normal(key, (FRAMES, POS, HEADS * HD), jnp.float32), -6.0, 6.0)
    return own_rows.astype(jnp.bfloat16)


def draw_head_class(key, part):
    key = jax.random.fold_in(key, 3)
    shuffled = jax.random.permutation(key, HEADS)
    return (shuffled >= HEADS - TEMP_HEADS).astype(jnp.int32)


def level_of(rng, dims, pieces, smallest, top_value):
    gain, own = 1.0, jax.random.fold_in(rng, 6)
    for position, shards_of in pieces:
        steps = jnp.exp(jax.random.uniform(jax.random.fold_in(own, position), (shards_of,), jnp.float32, smallest / len(pieces), top_value / len(pieces)))
        gain = gain * jnp.repeat(steps, dims[position] // shards_of).reshape([-1 if axis == position else 1 for axis in range(len(dims))])
    return gain


def bell_draw(stream_key, shape, spread, bound, cuts=(), held_as=jnp.bfloat16):
    entries = jax.random.normal(stream_key, shape, jnp.float32) * spread
    if len(cuts) > 0:
        entries = level_of(stream_key, shape, cuts, -0.22, 0.18) * entries
    return jnp.clip(entries, min=-bound, max=bound).astype(held_as)


def setup_inputs(seed: int = 0) -> dict:
    streams_of = jax.random.split(jax.random.key(seed), 6)
    query = draw_query(jax.random.fold_in(streams_of[5], 71), 0)
    key_proj = draw_key_proj(jax.random.fold_in(streams_of[5], 71), 0)
    value = bell_draw(streams_of[2], (FRAMES, POS, HEADS * HD), 1.0, 6.0, ((0, 16), (1, 8)))
    head_class = draw_head_class(jax.random.fold_in(streams_of[5], 71), 0)
    frame_count = jax.random.randint(streams_of[4], (1,), FRAMES - 4 * FR_DEV, FRAMES).astype(jnp.int32)
    return {"query": query, "key_proj": key_proj, "value": value, "head_class": head_class, "frame_count": frame_count}


def spatial_frame(items):
    queries, key_rows, value_rows = items
    scale = HD ** -0.5
    scores = jnp.einsum("qhd,khd->hqk", queries.astype(jnp.float32), key_rows.astype(jnp.float32)) * scale
    weights = jnp.exp(scores - jnp.max(scores, axis=-1, keepdims=True))
    weights = weights / jnp.sum(weights, axis=-1, keepdims=True)
    return jnp.einsum("hqk,khd->qhd", weights, value_rows.astype(jnp.float32))


def reference(query, key_proj, value, head_class, frame_count):
    head_order = jnp.argsort(head_class, stable=True).astype(jnp.int32)
    inverse = jnp.argsort(head_order, stable=True).astype(jnp.int32)
    frame_limit = frame_count[0]
    shape_four = (FRAMES, POS, HEADS, HD)
    query_four = query.reshape(shape_four)
    key_four = key_proj.reshape(shape_four)
    value_four = value.reshape(shape_four)
    spatial_heads = head_order[:HEADS - TEMP_HEADS]
    temporal_heads = head_order[HEADS - TEMP_HEADS:]
    spatial_part = lax.map(spatial_frame, (jnp.take(query_four, spatial_heads, axis=2),
                                           jnp.take(key_four, spatial_heads, axis=2),
                                           jnp.take(value_four, spatial_heads, axis=2)))
    query_time = jnp.take(query_four, temporal_heads, axis=2).astype(jnp.float32)
    key_time = jnp.take(key_four, temporal_heads, axis=2).astype(jnp.float32)
    value_time = jnp.take(value_four, temporal_heads, axis=2).astype(jnp.float32)
    scores = jnp.einsum("fphd,gphd->phfg", query_time, key_time) * (HD ** -0.5)
    valid = jnp.arange(FRAMES, dtype=jnp.int32) < frame_limit
    scores = jnp.where(valid, scores, -jnp.inf)
    weights = jnp.exp(scores - jnp.max(scores, axis=-1, keepdims=True))
    weights = weights / jnp.sum(weights, axis=-1, keepdims=True)
    temporal_part = jnp.einsum("phfg,gphd->fphd", weights, value_time)
    joined = jnp.concatenate([spatial_part, temporal_part], axis=2)
    restored = jnp.take(joined, inverse, axis=2)
    live = jnp.arange(FRAMES, dtype=jnp.int32) < frame_limit
    restored = jnp.where(live[:, None, None, None], restored, jnp.zeros_like(restored))
    return restored.reshape(FRAMES, POS, HEADS * HD).astype(jnp.bfloat16)
```

```python
import functools

import jax
import jax.numpy as jnp
from jax import lax
from jax.experimental import pallas as pl
from jax.experimental.pallas import tpu as pltpu
from jax.sharding import PartitionSpec as P

HEADS = 24
TEMP_HEADS = 8
SPACE_HEADS = HEADS - TEMP_HEADS
HD = 128
FR = 2
ROWS = 256
TM = 16
SPACE = 8
UNITS = 4
HALF = ROWS // 2
GROUP = 16
LOG2E = 1.4426950408889634
EXP_SCALE = HD**-0.5 * LOG2E
MASKED = -1e30
MESH = pl.DeviceIdType.MESH
CONTRACT_LAST = (((1,), (1,)), ((), ()))


def softmax_parts(scores):
    peak = jnp.max(scores, axis=-1, keepdims=True)
    weights = jnp.exp2((scores - peak) * EXP_SCALE)
    return weights.astype(jnp.bfloat16), jnp.sum(weights, axis=-1, keepdims=True)


def attend_kernel(
    order_ref, count_ref, q_ref, k_ref, v_ref, r_ref,
    stage, recv, t_stage, t_recv, out_stage, t_out,
    fwd_send, fwd_recv, t_send, t_recv_sem, back_send, back_recv, tb_send, tb_recv, local_sem, t_local_sem,
):
    tm = lax.axis_index("tm")
    space = lax.axis_index("space")
    tensors = (q_ref, k_ref, v_ref)

    def space_peer(step):
        return lax.rem(space // 2 + step // 2, 4) * 2 + lax.rem(space + step, 2)

    def tm_peer(step):
        high = lax.rem(tm // 8 + step // 8, 2)
        depth = lax.rem(tm // 2 + step // 2, 4)
        return (high * 4 + depth) * 2 + lax.rem(tm + step, 2)

    def fwd_copy(unit, peer, slot):
        return pltpu.make_async_remote_copy(
            src_ref=stage.at[unit, peer], dst_ref=recv.at[unit, slot],
            send_sem=fwd_send.at[unit, peer], recv_sem=fwd_recv.at[unit, slot],
            device_id=(tm, peer), device_id_type=MESH,
        )

    def back_copy(unit, peer, owner):
        return pltpu.make_async_remote_copy(
            src_ref=out_stage.at[unit, peer],
            dst_ref=r_ref.at[2 * owner + unit // 2, lax.rem(unit, 2)],
            send_sem=back_send.at[unit, peer], recv_sem=back_recv.at[unit, owner],
            device_id=(tm, peer), device_id_type=MESH,
        )

    def t_copy(peer, slot):
        return pltpu.make_async_remote_copy(
            src_ref=t_stage.at[peer], dst_ref=t_recv.at[slot],
            send_sem=t_send.at[peer], recv_sem=t_recv_sem.at[slot],
            device_id=(peer, space), device_id_type=MESH,
        )

    def t_back_copy(peer, owner):
        return pltpu.make_async_remote_copy(
            src_ref=t_out.at[peer],
            dst_ref=r_ref.at[SPACE_HEADS + owner // 2, :, pl.ds(HALF * lax.rem(owner, 2), HALF)],
            send_sem=tb_send.at[peer], recv_sem=tb_recv.at[owner],
            device_id=(peer, space), device_id_type=MESH,
        )

    barrier = pltpu.get_barrier_semaphore()

    def greet_space(step, carry):
        pl.semaphore_signal(barrier, inc=1, device_id=(tm, space_peer(step)), device_id_type=MESH)
        return carry

    def greet_tm(step, carry):
        pl.semaphore_signal(barrier, inc=1, device_id=(tm_peer(step), space), device_id_type=MESH)
        return carry

    lax.fori_loop(1, SPACE, greet_space, 0)
    lax.fori_loop(1, TM, greet_tm, 0)

    def stage_unit(unit):
        frame = lax.rem(unit, 2)

        def one(step, carry):
            peer = space_peer(step)
            head = order_ref[2 * peer + unit // 2]
            lanes = pl.ds(head * HD, HD)
            for index, tensor in enumerate(tensors):
                stage[unit, peer, index] = tensor[frame, :, lanes]
            return carry

        lax.fori_loop(0, SPACE, one, 0)

    def send_unit(unit):
        def one(step, carry):
            peer = space_peer(step)
            fwd_copy(unit, peer, space).start()
            return carry

        lax.fori_loop(1, SPACE, one, 0)
        recv[unit, space] = stage[unit, space]

    def stage_temporal():
        def one(step, carry):
            head = order_ref[SPACE_HEADS + step]
            lanes = pl.ds(head * HD, HD)
            for index, tensor in enumerate(tensors):
                for half in range(2):
                    t_stage[2 * step + half, index] = tensor[:, half * HALF:(half + 1) * HALF, lanes]
            return carry

        lax.fori_loop(0, TEMP_HEADS, one, 0)

    def send_temporal():
        def one(step, carry):
            t_copy(tm_peer(step), tm).start()
            return carry

        lax.fori_loop(1, TM, one, 0)
        t_recv[tm] = t_stage[tm]

    stage_unit(0)
    pl.semaphore_wait(barrier, SPACE + TM - 2)
    send_unit(0)
    stage_temporal()
    send_temporal()

    def later_unit(unit, carry):
        stage_unit(unit)
        send_unit(unit)
        return carry

    lax.fori_loop(1, UNITS, later_unit, 0)

    def attend_unit(unit):
        def arrived(step, carry):
            peer = space_peer(step)
            fwd_copy(unit, peer, peer).wait_recv()
            return carry

        lax.fori_loop(1, SPACE, arrived, 0)

        def block(step, carry):
            peer = space_peer(lax.rem(step + 1, SPACE))
            keys = recv[unit, :, 1].reshape(SPACE * ROWS, HD)
            values = recv[unit, :, 2].reshape(SPACE * ROWS, HD)
            scores = lax.dot_general(
                recv[unit, peer, 0], keys, CONTRACT_LAST, preferred_element_type=jnp.float32
            )
            weights, total = softmax_parts(scores)
            mixed = jnp.dot(weights, values, preferred_element_type=jnp.float32)
            out_stage[unit, peer] = (mixed / total).astype(jnp.bfloat16)

            @pl.when(step < SPACE - 1)
            def _():
                back_copy(unit, peer, space).start()

            return carry

        lax.fori_loop(0, SPACE, block, 0)
        pltpu.make_async_copy(
            out_stage.at[unit, space], r_ref.at[2 * space + unit // 2, lax.rem(unit, 2)], local_sem.at[unit]
        ).start()

    def attend_temporal():
        def arrived(step, carry):
            peer = tm_peer(step)
            t_copy(peer, peer).wait_recv()
            return carry

        lax.fori_loop(1, TM, arrived, 0)
        width = TM * FR * GROUP
        row = lax.broadcasted_iota(jnp.int32, (width, width), 0)
        column = lax.broadcasted_iota(jnp.int32, (width, width), 1)
        same = (row % GROUP) == (column % GROUP)
        allowed = same & (column < count_ref[0] * GROUP)

        def group(index, carry):
            span = pl.ds(pl.multiple_of(index * GROUP, GROUP), GROUP)
            queries = t_recv[:, 0, :, span].reshape(width, HD)
            keys = t_recv[:, 1, :, span].reshape(width, HD)
            values = t_recv[:, 2, :, span].reshape(width, HD)
            scores = lax.dot_general(queries, keys, CONTRACT_LAST, preferred_element_type=jnp.float32)
            weights, total = softmax_parts(jnp.where(allowed, scores, MASKED))
            mixed = jnp.dot(weights, values, preferred_element_type=jnp.float32)
            t_out[:, :, span] = (mixed / total).astype(jnp.bfloat16).reshape(TM, FR, GROUP, HD)
            return carry

        lax.fori_loop(0, HALF // GROUP, group, 0)

        def back(step, carry):
            t_back_copy(tm_peer(step), tm).start()
            return carry

        lax.fori_loop(1, TM, back, 0)
        pltpu.make_async_copy(
            t_out.at[tm], r_ref.at[SPACE_HEADS + tm // 2, :, pl.ds(HALF * lax.rem(tm, 2), HALF)], t_local_sem
        ).start()

    attend_unit(0)
    attend_temporal()

    def attend_later(unit, carry):
        attend_unit(unit)
        return carry

    lax.fori_loop(1, UNITS, attend_later, 0)

    def finish_unit(unit, carry):
        def one(step, inner):
            peer = space_peer(step)
            fwd_copy(unit, peer, space).wait_send()
            back_copy(unit, peer, space).wait_send()
            back_copy(unit, peer, peer).wait_recv()
            return inner

        lax.fori_loop(1, SPACE, one, 0)
        pltpu.make_async_copy(
            out_stage.at[unit, space], r_ref.at[2 * space + unit // 2, lax.rem(unit, 2)], local_sem.at[unit]
        ).wait()
        return carry

    lax.fori_loop(0, UNITS, finish_unit, 0)

    def finish_temporal(step, carry):
        peer = tm_peer(step)
        t_copy(peer, tm).wait_send()
        t_back_copy(peer, tm).wait_send()
        t_back_copy(peer, peer).wait_recv()
        return carry

    lax.fori_loop(1, TM, finish_temporal, 0)
    pltpu.make_async_copy(
        t_out.at[tm], r_ref.at[SPACE_HEADS + tm // 2, :, pl.ds(HALF * lax.rem(tm, 2), HALF)], t_local_sem
    ).wait()


def restore_kernel(inverse_ref, count_ref, r_ref, out_ref):
    first = lax.axis_index("tm") * FR
    for frame in range(FR):
        live = first + frame < count_ref[0]
        for head in range(HEADS):
            rows = r_ref[inverse_ref[head], frame]
            out_ref[frame, :, head * HD:(head + 1) * HD] = jnp.where(live, rows, jnp.zeros_like(rows))


def attend_call(order, frame_count, query, key_proj, value):
    block = (ROWS, HD)
    smem = pl.BlockSpec(memory_space=pltpu.SMEM)
    vmem = pl.BlockSpec(memory_space=pltpu.VMEM)
    return pl.pallas_call(
        attend_kernel,
        out_shape=jax.ShapeDtypeStruct((HEADS, FR) + block, jnp.bfloat16),
        in_specs=[smem, smem, vmem, vmem, vmem],
        out_specs=pl.BlockSpec(memory_space=pl.ANY),
        scratch_shapes=[
            pltpu.VMEM((UNITS, SPACE, 3) + block, jnp.bfloat16),
            pltpu.VMEM((UNITS, SPACE, 3) + block, jnp.bfloat16),
            pltpu.VMEM((TM, 3, FR, HALF, HD), jnp.bfloat16),
            pltpu.VMEM((TM, 3, FR, HALF, HD), jnp.bfloat16),
            pltpu.VMEM((UNITS, SPACE) + block, jnp.bfloat16),
            pltpu.VMEM((TM, FR, HALF, HD), jnp.bfloat16),
            pltpu.SemaphoreType.DMA((UNITS, SPACE)),
            pltpu.SemaphoreType.DMA((UNITS, SPACE)),
            pltpu.SemaphoreType.DMA((TM,)),
            pltpu.SemaphoreType.DMA((TM,)),
            pltpu.SemaphoreType.DMA((UNITS, SPACE)),
            pltpu.SemaphoreType.DMA((UNITS, SPACE)),
            pltpu.SemaphoreType.DMA((TM,)),
            pltpu.SemaphoreType.DMA((TM,)),
            pltpu.SemaphoreType.DMA((UNITS,)),
            pltpu.SemaphoreType.DMA,
        ],
        compiler_params=pltpu.CompilerParams(
            collective_id=0, has_side_effects=True, vmem_limit_bytes=52 * 2**20
        ),
        name="attend",
    )(order, frame_count, query, key_proj, value)


def restore_call(inverse, frame_count, results):
    step_rows = 64
    return pl.pallas_call(
        restore_kernel,
        out_shape=jax.ShapeDtypeStruct((FR, ROWS, HEADS * HD), jnp.bfloat16),
        grid=(ROWS // step_rows,),
        in_specs=[
            pl.BlockSpec(memory_space=pltpu.SMEM),
            pl.BlockSpec(memory_space=pltpu.SMEM),
            pl.BlockSpec((HEADS, FR, step_rows, HD), lambda i: (0, 0, i, 0)),
        ],
        out_specs=pl.BlockSpec((FR, step_rows, HEADS * HD), lambda i: (0, i, 0)),
        compiler_params=pltpu.CompilerParams(vmem_limit_bytes=16 * 2**20),
        name="restore",
    )(inverse, frame_count, results)


def on_device(query, key_proj, value, head_class, frame_count):
    heads = jnp.arange(HEADS, dtype=jnp.int32)
    earlier = heads[None, :] < heads[:, None]
    alike = head_class[None, :] == head_class[:, None]
    inverse = jnp.sum((earlier & alike).astype(jnp.int32), axis=1) + SPACE_HEADS * head_class
    order = jnp.sum(jnp.where(inverse[None, :] == heads[:, None], heads[None, :], 0), axis=1)
    results = attend_call(order, frame_count, query, key_proj, value)
    return restore_call(inverse, frame_count, results)


def solution(mesh):
    return jax.shard_map(
        on_device,
        mesh=mesh,
        in_specs=(P("tm", "space", None), P("tm", "space", None), P("tm", "space", None), P(), P()),
        out_specs=P("tm", "space", None),
        check_vma=False,
    )
```

```python
import functools

import jax
import jax.numpy as jnp
from jax import lax
from jax.experimental import pallas as pl
from jax.experimental.pallas import tpu as pltpu
from jax.sharding import PartitionSpec as P

HEADS = 24
TEMP_HEADS = 8
SPACE_HEADS = HEADS - TEMP_HEADS
HD = 128
FR = 2
ROWS = 256
TM = 16
SPACE = 8
UNITS = 4
HALF = ROWS // 2
GROUP = 16
STEP_ROWS = 64
LOG2E = 1.4426950408889634
EXP_SCALE = HD**-0.5 * LOG2E
MASKED = -1e30
MESH = pl.DeviceIdType.MESH
CONTRACT_LAST = (((1,), (1,)), ((), ()))


def softmax_parts(scores):
    peak = jnp.max(scores, axis=-1, keepdims=True)
    weights = jnp.exp2((scores - peak) * EXP_SCALE)
    return weights.astype(jnp.bfloat16), jnp.sum(weights, axis=-1, keepdims=True)


def head_places(class_ref):
    places, spatial, temporal = [], jnp.int32(0), jnp.int32(SPACE_HEADS)
    for head in range(HEADS):
        kind = class_ref[head]
        places.append(jnp.where(kind == 0, spatial, temporal))
        spatial = spatial + (1 - kind)
        temporal = temporal + kind
    return places


def attend_kernel(
    class_ref, count_ref, q_ref, k_ref, v_ref, r_ref,
    held_first, held_second, order_ref, load_sem, stage, recv, t_stage, t_recv, out_stage, t_out,
    fwd_send, fwd_recv, t_send, t_recv_sem, back_send, back_recv, tb_send, tb_recv, local_sem, t_local_sem,
):
    tm = lax.axis_index("tm")
    space = lax.axis_index("space")
    tensors = (q_ref, k_ref, v_ref)
    held = (held_first, held_second)

    def load_copy(frame, index):
        return pltpu.make_async_copy(tensors[index].at[frame], held[frame].at[index], load_sem.at[frame, index])

    for frame in range(FR):
        for index in range(3):
            load_copy(frame, index).start()

    def space_peer(step):
        return lax.rem(space // 2 + step // 2, 4) * 2 + lax.rem(space + step, 2)

    def tm_peer(step):
        high = lax.rem(tm // 8 + step // 8, 2)
        depth = lax.rem(tm // 2 + step // 2, 4)
        return (high * 4 + depth) * 2 + lax.rem(tm + step, 2)

    def fwd_copy(unit, peer, slot):
        return pltpu.make_async_remote_copy(
            src_ref=stage.at[unit, peer], dst_ref=recv.at[unit, slot],
            send_sem=fwd_send.at[unit, peer], recv_sem=fwd_recv.at[unit, slot],
            device_id=(tm, peer), device_id_type=MESH,
        )

    def back_copy(unit, peer, owner):
        return pltpu.make_async_remote_copy(
            src_ref=out_stage.at[unit, peer],
            dst_ref=r_ref.at[2 * owner + unit // 2, lax.rem(unit, 2)],
            send_sem=back_send.at[unit, peer], recv_sem=back_recv.at[unit, owner],
            device_id=(tm, peer), device_id_type=MESH,
        )

    def t_copy(peer, slot):
        return pltpu.make_async_remote_copy(
            src_ref=t_stage.at[peer], dst_ref=t_recv.at[slot],
            send_sem=t_send.at[peer], recv_sem=t_recv_sem.at[slot],
            device_id=(peer, space), device_id_type=MESH,
        )

    def t_back_copy(peer, owner):
        return pltpu.make_async_remote_copy(
            src_ref=t_out.at[peer],
            dst_ref=r_ref.at[SPACE_HEADS + owner // 2, :, pl.ds(HALF * lax.rem(owner, 2), HALF)],
            send_sem=tb_send.at[peer], recv_sem=tb_recv.at[owner],
            device_id=(peer, space), device_id_type=MESH,
        )

    barrier = pltpu.get_barrier_semaphore()

    def greet_space(step, carry):
        pl.semaphore_signal(barrier, inc=1, device_id=(tm, space_peer(step)), device_id_type=MESH)
        return carry

    def greet_tm(step, carry):
        pl.semaphore_signal(barrier, inc=1, device_id=(tm_peer(step), space), device_id_type=MESH)
        return carry

    lax.fori_loop(1, SPACE, greet_space, 0)
    lax.fori_loop(1, TM, greet_tm, 0)

    def stage_unit(unit):
        def one(step, carry):
            peer = space_peer(step)
            head = order_ref[2 * peer + unit // 2]
            lanes = pl.ds(head * HD, HD)
            for index in range(3):
                stage[unit, peer, index] = held[unit % 2][index, :, lanes]
            return carry

        lax.fori_loop(0, SPACE, one, 0)

    def send_unit(unit):
        def one(step, carry):
            peer = space_peer(step)
            fwd_copy(unit, peer, space).start()
            return carry

        lax.fori_loop(1, SPACE, one, 0)
        recv[unit, space] = stage[unit, space]

    def stage_temporal():
        def one(step, carry):
            head = order_ref[SPACE_HEADS + step]
            lanes = pl.ds(head * HD, HD)
            for index in range(3):
                for half in range(2):
                    for frame in range(FR):
                        t_stage[2 * step + half, index, frame] = held[frame][index, half * HALF:(half + 1) * HALF, lanes]
            return carry

        lax.fori_loop(0, TEMP_HEADS, one, 0)

    def send_temporal():
        def one(step, carry):
            t_copy(tm_peer(step), tm).start()
            return carry

        lax.fori_loop(1, TM, one, 0)
        t_recv[tm] = t_stage[tm]

    places = head_places(class_ref)
    for place in range(HEADS):
        order_ref[place] = sum(jnp.where(places[head] == place, head, 0) for head in range(HEADS))
    for index in range(3):
        load_copy(0, index).wait()
    stage_unit(0)
    pl.semaphore_wait(barrier, SPACE + TM - 2)
    send_unit(0)
    for index in range(3):
        load_copy(1, index).wait()
    stage_temporal()
    send_temporal()

    for unit in range(1, UNITS):
        stage_unit(unit)
        send_unit(unit)

    def attend_unit(unit):
        def arrived(step, carry):
            peer = space_peer(step)
            fwd_copy(unit, peer, peer).wait_recv()
            return carry

        lax.fori_loop(1, SPACE, arrived, 0)

        def block(step, carry):
            peer = space_peer(lax.rem(step + 1, SPACE))
            keys = recv[unit, :, 1].reshape(SPACE * ROWS, HD)
            values = recv[unit, :, 2].reshape(SPACE * ROWS, HD)
            scores = lax.dot_general(
                recv[unit, peer, 0], keys, CONTRACT_LAST, preferred_element_type=jnp.float32
            )
            weights, total = softmax_parts(scores)
            mixed = jnp.dot(weights, values, preferred_element_type=jnp.float32)
            out_stage[unit, peer] = (mixed / total).astype(jnp.bfloat16)

            @pl.when(step < SPACE - 1)
            def _():
                back_copy(unit, peer, space).start()

            return carry

        lax.fori_loop(0, SPACE, block, 0)
        pltpu.make_async_copy(
            out_stage.at[unit, space], r_ref.at[2 * space + unit // 2, lax.rem(unit, 2)], local_sem.at[unit]
        ).start()

    def attend_temporal():
        def arrived(step, carry):
            peer = tm_peer(step)
            t_copy(peer, peer).wait_recv()
            return carry

        lax.fori_loop(1, TM, arrived, 0)
        width = TM * FR * GROUP
        row = lax.broadcasted_iota(jnp.int32, (width, width), 0)
        column = lax.broadcasted_iota(jnp.int32, (width, width), 1)
        same = (row % GROUP) == (column % GROUP)
        allowed = same & (column < count_ref[0] * GROUP)

        def group(index, carry):
            span = pl.ds(pl.multiple_of(index * GROUP, GROUP), GROUP)
            queries = t_recv[:, 0, :, span].reshape(width, HD)
            keys = t_recv[:, 1, :, span].reshape(width, HD)
            values = t_recv[:, 2, :, span].reshape(width, HD)
            scores = lax.dot_general(queries, keys, CONTRACT_LAST, preferred_element_type=jnp.float32)
            weights, total = softmax_parts(jnp.where(allowed, scores, MASKED))
            mixed = jnp.dot(weights, values, preferred_element_type=jnp.float32)
            t_out[:, :, span] = (mixed / total).astype(jnp.bfloat16).reshape(TM, FR, GROUP, HD)
            return carry

        lax.fori_loop(0, HALF // GROUP, group, 0)

        def back(step, carry):
            t_back_copy(tm_peer(step), tm).start()
            return carry

        lax.fori_loop(1, TM, back, 0)
        pltpu.make_async_copy(
            t_out.at[tm], r_ref.at[SPACE_HEADS + tm // 2, :, pl.ds(HALF * lax.rem(tm, 2), HALF)], t_local_sem
        ).start()

    attend_unit(0)
    attend_temporal()

    def attend_later(unit, carry):
        attend_unit(unit)
        return carry

    lax.fori_loop(1, UNITS, attend_later, 0)

    def finish_unit(unit, carry):
        def one(step, inner):
            peer = space_peer(step)
            fwd_copy(unit, peer, space).wait_send()
            back_copy(unit, peer, space).wait_send()
            back_copy(unit, peer, peer).wait_recv()
            return inner

        lax.fori_loop(1, SPACE, one, 0)
        pltpu.make_async_copy(
            out_stage.at[unit, space], r_ref.at[2 * space + unit // 2, lax.rem(unit, 2)], local_sem.at[unit]
        ).wait()
        return carry

    lax.fori_loop(0, UNITS, finish_unit, 0)

    def finish_temporal(step, carry):
        peer = tm_peer(step)
        t_copy(peer, tm).wait_send()
        t_back_copy(peer, tm).wait_send()
        t_back_copy(peer, peer).wait_recv()
        return carry

    lax.fori_loop(1, TM, finish_temporal, 0)
    pltpu.make_async_copy(
        t_out.at[tm], r_ref.at[SPACE_HEADS + tm // 2, :, pl.ds(HALF * lax.rem(tm, 2), HALF)], t_local_sem
    ).wait()


def restore_kernel(class_ref, count_ref, r_ref, out_ref):
    first = lax.axis_index("tm") * FR
    places = head_places(class_ref)
    row = pl.multiple_of(pl.program_id(0) * STEP_ROWS, STEP_ROWS)
    for frame in range(FR):
        live = first + frame < count_ref[0]
        for head in range(HEADS):
            rows = r_ref[places[head], frame, pl.ds(row, STEP_ROWS)]
            out_ref[frame, :, head * HD:(head + 1) * HD] = jnp.where(live, rows, jnp.zeros_like(rows))


def attend_call(head_class, frame_count, query, key_proj, value):
    block = (ROWS, HD)
    smem = pl.BlockSpec(memory_space=pltpu.SMEM)
    hbm = pl.BlockSpec(memory_space=pltpu.HBM)
    return pl.pallas_call(
        attend_kernel,
        out_shape=pltpu.VMEM((HEADS, FR) + block, jnp.bfloat16),
        in_specs=[smem, smem, hbm, hbm, hbm],
        out_specs=pl.BlockSpec(memory_space=pltpu.VMEM),
        scratch_shapes=[
            pltpu.VMEM((3, ROWS, HEADS * HD), jnp.bfloat16),
            pltpu.VMEM((3, ROWS, HEADS * HD), jnp.bfloat16),
            pltpu.SMEM((HEADS,), jnp.int32),
            pltpu.SemaphoreType.DMA((FR, 3)),
            pltpu.VMEM((UNITS, SPACE, 3) + block, jnp.bfloat16),
            pltpu.VMEM((UNITS, SPACE, 3) + block, jnp.bfloat16),
            pltpu.VMEM((TM, 3, FR, HALF, HD), jnp.bfloat16),
            pltpu.VMEM((TM, 3, FR, HALF, HD), jnp.bfloat16),
            pltpu.VMEM((UNITS, SPACE) + block, jnp.bfloat16),
            pltpu.VMEM((TM, FR, HALF, HD), jnp.bfloat16),
            pltpu.SemaphoreType.DMA((UNITS, SPACE)),
            pltpu.SemaphoreType.DMA((UNITS, SPACE)),
            pltpu.SemaphoreType.DMA((TM,)),
            pltpu.SemaphoreType.DMA((TM,)),
            pltpu.SemaphoreType.DMA((UNITS, SPACE)),
            pltpu.SemaphoreType.DMA((UNITS, SPACE)),
            pltpu.SemaphoreType.DMA((TM,)),
            pltpu.SemaphoreType.DMA((TM,)),
            pltpu.SemaphoreType.DMA((UNITS,)),
            pltpu.SemaphoreType.DMA,
        ],
        compiler_params=pltpu.CompilerParams(
            collective_id=0, has_side_effects=True, vmem_limit_bytes=52 * 2**20
        ),
        name="attend",
    )(head_class, frame_count, query, key_proj, value)


def restore_call(head_class, frame_count, results):
    return pl.pallas_call(
        restore_kernel,
        out_shape=jax.ShapeDtypeStruct((FR, ROWS, HEADS * HD), jnp.bfloat16),
        grid=(ROWS // STEP_ROWS,),
        in_specs=[
            pl.BlockSpec(memory_space=pltpu.SMEM),
            pl.BlockSpec(memory_space=pltpu.SMEM),
            pl.BlockSpec(memory_space=pltpu.VMEM),
        ],
        out_specs=pl.BlockSpec((FR, STEP_ROWS, HEADS * HD), lambda i: (0, i, 0)),
        compiler_params=pltpu.CompilerParams(vmem_limit_bytes=16 * 2**20),
        name="restore",
    )(head_class, frame_count, pltpu.with_memory_space_constraint(results, pltpu.VMEM))


def on_device(query, key_proj, value, head_class, frame_count):
    results = attend_call(head_class, frame_count, query, key_proj, value)
    return restore_call(head_class, frame_count, results)


def solution(mesh):
    return jax.shard_map(
        on_device,
        mesh=mesh,
        in_specs=(P("tm", "space", None), P("tm", "space", None), P("tm", "space", None), P(), P()),
        out_specs=P("tm", "space", None),
        check_vma=False,
    )
```

```python
import functools

import jax
import jax.numpy as jnp
from jax import lax
from jax.experimental import pallas as pl
from jax.experimental.pallas import tpu as pltpu
from jax.sharding import PartitionSpec as P

HEADS = 24
TEMP_HEADS = 8
SPACE_HEADS = HEADS - TEMP_HEADS
HD = 128
FR = 2
ROWS = 256
TM = 16
SPACE = 8
UNITS = 4
HALF = ROWS // 2
GROUP = 16
LOG2E = 1.4426950408889634
EXP_SCALE = HD**-0.5 * LOG2E
MASKED = -1e30
MESH = pl.DeviceIdType.MESH
CONTRACT_LAST = (((1,), (1,)), ((), ()))


def softmax_parts(scores):
    peak = jnp.max(scores, axis=-1, keepdims=True)
    weights = jnp.exp2((scores - peak) * EXP_SCALE)
    return weights.astype(jnp.bfloat16), jnp.sum(weights, axis=-1, keepdims=True)


def head_places(class_ref):
    places, spatial, temporal = [], jnp.int32(0), jnp.int32(SPACE_HEADS)
    for head in range(HEADS):
        kind = class_ref[head]
        places.append(jnp.where(kind == 0, spatial, temporal))
        spatial = spatial + (1 - kind)
        temporal = temporal + kind
    return places


def attend_kernel(
    class_ref, count_ref, q_ref, k_ref, v_ref, out_ref,
    r_ref, held_first, held_second, order_ref, load_sem, stage, recv, t_stage, t_recv, out_stage, t_out,
    fwd_send, fwd_recv, t_send, t_recv_sem, back_send, back_recv, tb_send, tb_recv, local_sem, t_local_sem,
):
    tm = lax.axis_index("tm")
    space = lax.axis_index("space")
    tensors = (q_ref, k_ref, v_ref)
    held = (held_first, held_second)

    def load_copy(frame, index):
        return pltpu.make_async_copy(tensors[index].at[frame], held[frame].at[index], load_sem.at[frame, index])

    for index in range(3):
        load_copy(0, index).start()

    def space_peer(step):
        return lax.rem(space // 2 + step // 2, 4) * 2 + lax.rem(space + step, 2)

    def tm_peer(step):
        high = lax.rem(tm // 8 + step // 8, 2)
        depth = lax.rem(tm // 2 + step // 2, 4)
        return (high * 4 + depth) * 2 + lax.rem(tm + step, 2)

    def fwd_copy(unit, peer, slot):
        return pltpu.make_async_remote_copy(
            src_ref=stage.at[unit, peer], dst_ref=recv.at[unit, slot],
            send_sem=fwd_send.at[unit, peer], recv_sem=fwd_recv.at[unit, slot],
            device_id=(tm, peer), device_id_type=MESH,
        )

    def back_copy(unit, peer, owner):
        return pltpu.make_async_remote_copy(
            src_ref=out_stage.at[unit, peer],
            dst_ref=r_ref.at[2 * owner + unit // 2, lax.rem(unit, 2)],
            send_sem=back_send.at[unit, peer], recv_sem=back_recv.at[unit, owner],
            device_id=(tm, peer), device_id_type=MESH,
        )

    def t_copy(peer, slot):
        return pltpu.make_async_remote_copy(
            src_ref=t_stage.at[peer], dst_ref=t_recv.at[slot],
            send_sem=t_send.at[peer], recv_sem=t_recv_sem.at[slot],
            device_id=(peer, space), device_id_type=MESH,
        )

    def t_back_copy(peer, owner):
        return pltpu.make_async_remote_copy(
            src_ref=t_out.at[peer],
            dst_ref=r_ref.at[SPACE_HEADS + owner // 2, :, pl.ds(HALF * lax.rem(owner, 2), HALF)],
            send_sem=tb_send.at[peer], recv_sem=tb_recv.at[owner],
            device_id=(peer, space), device_id_type=MESH,
        )

    barrier = pltpu.get_barrier_semaphore()

    def greet_space(step, carry):
        pl.semaphore_signal(barrier, inc=1, device_id=(tm, space_peer(step)), device_id_type=MESH)
        return carry

    def greet_tm(step, carry):
        pl.semaphore_signal(barrier, inc=1, device_id=(tm_peer(step), space), device_id_type=MESH)
        return carry

    lax.fori_loop(1, SPACE, greet_space, 0)
    lax.fori_loop(1, TM, greet_tm, 0)

    def send_unit(unit):
        def pick(peer, refs):
            head = order_ref[2 * peer + unit // 2]
            lanes = pl.ds(head * HD, HD)
            for index in range(3):
                refs[index][...] = held[unit % 2][index, :, lanes]

        def one(step, carry):
            peer = space_peer(step)
            pick(peer, [stage.at[unit, peer, index] for index in range(3)])
            fwd_copy(unit, peer, space).start()
            return carry

        lax.fori_loop(1, SPACE, one, 0)
        pick(space, [recv.at[unit, space, index] for index in range(3)])

    def stage_temporal():
        def one(step, carry):
            head = order_ref[SPACE_HEADS + step]
            lanes = pl.ds(head * HD, HD)
            for index in range(3):
                for half in range(2):
                    for frame in range(FR):
                        t_stage[2 * step + half, index, frame] = held[frame][index, half * HALF:(half + 1) * HALF, lanes]
            return carry

        lax.fori_loop(0, TEMP_HEADS, one, 0)

    def send_temporal():
        def one(step, carry):
            t_copy(tm_peer(step), tm).start()
            return carry

        lax.fori_loop(1, TM, one, 0)
        t_recv[tm] = t_stage[tm]

    places = head_places(class_ref)
    for place in range(HEADS):
        order_ref[place] = sum(jnp.where(places[head] == place, head, 0) for head in range(HEADS))
    for index in range(3):
        load_copy(0, index).wait()
    for index in range(3):
        load_copy(1, index).start()
    pl.semaphore_wait(barrier, SPACE + TM - 2)
    send_unit(0)
    for index in range(3):
        load_copy(1, index).wait()
    stage_temporal()
    send_temporal()
    for unit in range(1, UNITS):
        send_unit(unit)

    def attend_unit(unit):
        def arrived(step, carry):
            peer = space_peer(step)
            fwd_copy(unit, peer, peer).wait_recv()
            return carry

        lax.fori_loop(1, SPACE, arrived, 0)

        def block(step, carry):
            peer = space_peer(lax.rem(step + 1, SPACE))
            keys = recv[unit, :, 1].reshape(SPACE * ROWS, HD)
            values = recv[unit, :, 2].reshape(SPACE * ROWS, HD)
            scores = lax.dot_general(
                recv[unit, peer, 0], keys, CONTRACT_LAST, preferred_element_type=jnp.float32
            )
            weights, total = softmax_parts(scores)
            mixed = jnp.dot(weights, values, preferred_element_type=jnp.float32)
            out_stage[unit, peer] = (mixed / total).astype(jnp.bfloat16)

            @pl.when(step < SPACE - 1)
            def _():
                back_copy(unit, peer, space).start()

            return carry

        lax.fori_loop(0, SPACE, block, 0)
        pltpu.make_async_copy(
            out_stage.at[unit, space], r_ref.at[2 * space + unit // 2, lax.rem(unit, 2)], local_sem.at[unit]
        ).start()

    def attend_temporal():
        def arrived(step, carry):
            peer = tm_peer(step)
            t_copy(peer, peer).wait_recv()
            return carry

        lax.fori_loop(1, TM, arrived, 0)
        width = TM * FR * GROUP
        row = lax.broadcasted_iota(jnp.int32, (width, width), 0)
        column = lax.broadcasted_iota(jnp.int32, (width, width), 1)
        same = (row % GROUP) == (column % GROUP)
        allowed = same & (column < count_ref[0] * GROUP)

        def group(index, carry):
            span = pl.ds(pl.multiple_of(index * GROUP, GROUP), GROUP)
            queries = t_recv[:, 0, :, span].reshape(width, HD)
            keys = t_recv[:, 1, :, span].reshape(width, HD)
            values = t_recv[:, 2, :, span].reshape(width, HD)
            scores = lax.dot_general(queries, keys, CONTRACT_LAST, preferred_element_type=jnp.float32)
            weights, total = softmax_parts(jnp.where(allowed, scores, MASKED))
            mixed = jnp.dot(weights, values, preferred_element_type=jnp.float32)
            t_out[:, :, span] = (mixed / total).astype(jnp.bfloat16).reshape(TM, FR, GROUP, HD)
            return carry

        lax.fori_loop(0, HALF // GROUP, group, 0)

        def back(step, carry):
            t_back_copy(tm_peer(step), tm).start()
            return carry

        lax.fori_loop(1, TM, back, 0)
        pltpu.make_async_copy(
            t_out.at[tm], r_ref.at[SPACE_HEADS + tm // 2, :, pl.ds(HALF * lax.rem(tm, 2), HALF)], t_local_sem
        ).start()

    attend_unit(0)
    attend_temporal()

    def attend_later(unit, carry):
        attend_unit(unit)
        return carry

    lax.fori_loop(1, UNITS, attend_later, 0)

    def finish_unit(unit, carry):
        def one(step, inner):
            peer = space_peer(step)
            fwd_copy(unit, peer, space).wait_send()
            back_copy(unit, peer, space).wait_send()
            back_copy(unit, peer, peer).wait_recv()
            return inner

        lax.fori_loop(1, SPACE, one, 0)
        pltpu.make_async_copy(
            out_stage.at[unit, space], r_ref.at[2 * space + unit // 2, lax.rem(unit, 2)], local_sem.at[unit]
        ).wait()
        return carry

    lax.fori_loop(0, UNITS, finish_unit, 0)

    def finish_temporal(step, carry):
        peer = tm_peer(step)
        t_copy(peer, tm).wait_send()
        t_back_copy(peer, tm).wait_send()
        t_back_copy(peer, peer).wait_recv()
        return carry

    lax.fori_loop(1, TM, finish_temporal, 0)
    pltpu.make_async_copy(
        t_out.at[tm], r_ref.at[SPACE_HEADS + tm // 2, :, pl.ds(HALF * lax.rem(tm, 2), HALF)], t_local_sem
    ).wait()

    for frame in range(FR):
        present = FR * tm + frame < count_ref[0]
        for head in range(HEADS):
            rows = r_ref[places[head], frame]
            out_ref[frame, :, head * HD:(head + 1) * HD] = jnp.where(present, rows, jnp.zeros_like(rows))


def attend_call(head_class, frame_count, query, key_proj, value):
    block = (ROWS, HD)
    smem = pl.BlockSpec(memory_space=pltpu.SMEM)
    hbm = pl.BlockSpec(memory_space=pltpu.HBM)
    return pl.pallas_call(
        attend_kernel,
        out_shape=pltpu.VMEM((FR, ROWS, HEADS * HD), jnp.bfloat16),
        in_specs=[smem, smem, hbm, hbm, hbm],
        out_specs=pl.BlockSpec(memory_space=pltpu.VMEM),
        scratch_shapes=[
            pltpu.VMEM((HEADS, FR) + block, jnp.bfloat16),
            pltpu.VMEM((3, ROWS, HEADS * HD), jnp.bfloat16),
            pltpu.VMEM((3, ROWS, HEADS * HD), jnp.bfloat16),
            pltpu.SMEM((HEADS,), jnp.int32),
            pltpu.SemaphoreType.DMA((FR, 3)),
            pltpu.VMEM((UNITS, SPACE, 3) + block, jnp.bfloat16),
            pltpu.VMEM((UNITS, SPACE, 3) + block, jnp.bfloat16),
            pltpu.VMEM((TM, 3, FR, HALF, HD), jnp.bfloat16),
            pltpu.VMEM((TM, 3, FR, HALF, HD), jnp.bfloat16),
            pltpu.VMEM((UNITS, SPACE) + block, jnp.bfloat16),
            pltpu.VMEM((TM, FR, HALF, HD), jnp.bfloat16),
            pltpu.SemaphoreType.DMA((UNITS, SPACE)),
            pltpu.SemaphoreType.DMA((UNITS, SPACE)),
            pltpu.SemaphoreType.DMA((TM,)),
            pltpu.SemaphoreType.DMA((TM,)),
            pltpu.SemaphoreType.DMA((UNITS, SPACE)),
            pltpu.SemaphoreType.DMA((UNITS, SPACE)),
            pltpu.SemaphoreType.DMA((TM,)),
            pltpu.SemaphoreType.DMA((TM,)),
            pltpu.SemaphoreType.DMA((UNITS,)),
            pltpu.SemaphoreType.DMA,
        ],
        compiler_params=pltpu.CompilerParams(
            collective_id=0, has_side_effects=True, vmem_limit_bytes=52 * 2**20
        ),
        name="attend",
    )(head_class, frame_count, query, key_proj, value)


def on_device(query, key_proj, value, head_class, frame_count):
    return attend_call(head_class, frame_count, query, key_proj, value)


def solution(mesh):
    return jax.shard_map(
        on_device,
        mesh=mesh,
        in_specs=(P("tm", "space", None), P("tm", "space", None), P("tm", "space", None), P(), P()),
        out_specs=P("tm", "space", None),
        check_vma=False,
    )
```

```python
import functools

import jax
import jax.numpy as jnp
from jax import lax
from jax.experimental import pallas as pl
from jax.experimental.pallas import tpu as pltpu
from jax.sharding import PartitionSpec as P

HEADS = 24
TEMP_HEADS = 8
SPACE_HEADS = HEADS - TEMP_HEADS
HD = 128
FR = 2
ROWS = 256
TM = 16
SPACE = 8
UNITS = 4
HALF = ROWS // 2
GROUP = 16
HUB = SPACE - 1
GATE = SPACE - 2
UNIT_ORDER = (0, 2, 1, 3)
LOG2E = 1.4426950408889634
EXP_SCALE = HD**-0.5 * LOG2E
MASKED = -1e30
MESH = pl.DeviceIdType.MESH
CONTRACT_LAST = (((1,), (1,)), ((), ()))


def softmax_parts(scores):
    peak = jnp.max(scores, axis=-1, keepdims=True)
    weights = jnp.exp2((scores - peak) * EXP_SCALE)
    return weights.astype(jnp.bfloat16), jnp.sum(weights, axis=-1, keepdims=True)


def head_places(class_ref):
    places, spatial, temporal = [], jnp.int32(0), jnp.int32(SPACE_HEADS)
    for head in range(HEADS):
        kind = class_ref[head]
        places.append(jnp.where(kind == 0, spatial, temporal))
        spatial = spatial + (1 - kind)
        temporal = temporal + kind
    return places


def attend_kernel(
    class_ref, count_ref, q_ref, k_ref, v_ref, out_ref,
    r_ref, held_first, held_second, order_ref, load_sem, stage, recv, t_stage, t_recv, out_stage, t_out,
    fwd_send, fwd_recv, t_send, t_recv_sem, back_send, back_recv, tb_send, tb_recv, local_sem, t_local_sem,
    space_go, tm_go,
):
    tm = lax.axis_index("tm")
    space = lax.axis_index("space")
    tensors = (q_ref, k_ref, v_ref)
    held = (held_first, held_second)

    def load_copy(frame, index):
        return pltpu.make_async_copy(tensors[index].at[frame], held[frame].at[index], load_sem.at[frame, index])

    for index in range(3):
        load_copy(0, index).start()

    def space_peer(step):
        return lax.rem(space // 2 + step // 2, 4) * 2 + lax.rem(space + step, 2)

    def tm_peer(step):
        high = lax.rem(tm // 8 + step // 8, 2)
        depth = lax.rem(tm // 2 + step // 2, 4)
        return (high * 4 + depth) * 2 + lax.rem(tm + step, 2)

    def fwd_copy(unit, peer, slot):
        return pltpu.make_async_remote_copy(
            src_ref=stage.at[unit, peer], dst_ref=recv.at[unit, slot],
            send_sem=fwd_send.at[unit, peer], recv_sem=fwd_recv.at[unit, slot],
            device_id=(tm, peer), device_id_type=MESH,
        )

    def back_copy(unit, peer, owner):
        return pltpu.make_async_remote_copy(
            src_ref=out_stage.at[unit, peer],
            dst_ref=r_ref.at[2 * owner + unit // 2, lax.rem(unit, 2)],
            send_sem=back_send.at[unit, peer], recv_sem=back_recv.at[unit, owner],
            device_id=(tm, peer), device_id_type=MESH,
        )

    def t_copy(peer, slot):
        return pltpu.make_async_remote_copy(
            src_ref=t_stage.at[peer], dst_ref=t_recv.at[slot],
            send_sem=t_send.at[peer], recv_sem=t_recv_sem.at[slot],
            device_id=(peer, space), device_id_type=MESH,
        )

    def t_back_copy(peer, owner):
        return pltpu.make_async_remote_copy(
            src_ref=t_out.at[peer],
            dst_ref=r_ref.at[SPACE_HEADS + owner // 2, :, pl.ds(HALF * lax.rem(owner, 2), HALF)],
            send_sem=tb_send.at[peer], recv_sem=tb_recv.at[owner],
            device_id=(peer, space), device_id_type=MESH,
        )

    barrier = pltpu.get_barrier_semaphore()

    def tell_space(sem, me):
        for other in range(SPACE):
            if other != me:
                pl.semaphore_signal(sem, inc=1, device_id=(tm, other), device_id_type=MESH)

    @pl.when(space != HUB)
    def _():
        pl.semaphore_signal(barrier, inc=1, device_id=(tm, HUB), device_id_type=MESH)

    @pl.when(space == HUB)
    def _():
        pl.semaphore_wait(barrier, SPACE - 1)
        tell_space(space_go, HUB)

    def meet_space():
        @pl.when(space != HUB)
        def _():
            pl.semaphore_wait(space_go, 1)

        @pl.when(space == GATE)
        def _():
            def greet(step, carry):
                pl.semaphore_signal(barrier, inc=1, device_id=(tm_peer(step), GATE), device_id_type=MESH)
                return carry

            lax.fori_loop(1, TM, greet, 0)

    def meet_tm():
        @pl.when(space == GATE)
        def _():
            pl.semaphore_wait(barrier, TM - 1)
            tell_space(tm_go, GATE)

        @pl.when(space != GATE)
        def _():
            pl.semaphore_wait(tm_go, 1)

    def send_unit(unit):
        def pick(peer, refs):
            head = order_ref[2 * peer + unit // 2]
            lanes = pl.ds(head * HD, HD)
            for index in range(3):
                refs[index][...] = held[unit % 2][index, :, lanes]

        def one(step, carry):
            peer = space_peer(step)
            pick(peer, [stage.at[unit, peer, index] for index in range(3)])
            fwd_copy(unit, peer, space).start()
            return carry

        lax.fori_loop(1, SPACE, one, 0)
        pick(space, [recv.at[unit, space, index] for index in range(3)])

    def stage_temporal():
        def one(step, carry):
            head = order_ref[SPACE_HEADS + step]
            lanes = pl.ds(head * HD, HD)
            for index in range(3):
                for half in range(2):
                    for frame in range(FR):
                        t_stage[2 * step + half, index, frame] = held[frame][index, half * HALF:(half + 1) * HALF, lanes]
            return carry

        lax.fori_loop(0, TEMP_HEADS, one, 0)

    def send_temporal():
        def one(step, carry):
            t_copy(tm_peer(step), tm).start()
            return carry

        lax.fori_loop(1, TM, one, 0)
        t_recv[tm] = t_stage[tm]

    places = head_places(class_ref)
    for place in range(HEADS):
        order_ref[place] = sum(jnp.where(places[head] == place, head, 0) for head in range(HEADS))
    for index in range(3):
        load_copy(0, index).wait()
    for index in range(3):
        load_copy(1, index).start()
    meet_space()
    def attend_unit(unit):
        def arrived(step, carry):
            peer = space_peer(step)
            fwd_copy(unit, peer, peer).wait_recv()
            return carry

        lax.fori_loop(1, SPACE, arrived, 0)

        def block(step, carry):
            peer = space_peer(lax.rem(step + 1, SPACE))
            keys = recv[unit, :, 1].reshape(SPACE * ROWS, HD)
            values = recv[unit, :, 2].reshape(SPACE * ROWS, HD)
            scores = lax.dot_general(
                recv[unit, peer, 0], keys, CONTRACT_LAST, preferred_element_type=jnp.float32
            )
            weights, total = softmax_parts(scores)
            mixed = jnp.dot(weights, values, preferred_element_type=jnp.float32)
            out_stage[unit, peer] = (mixed / total).astype(jnp.bfloat16)

            @pl.when(step < SPACE - 1)
            def _():
                back_copy(unit, peer, space).start()

            return carry

        lax.fori_loop(0, SPACE, block, 0)
        pltpu.make_async_copy(
            out_stage.at[unit, space], r_ref.at[2 * space + unit // 2, lax.rem(unit, 2)], local_sem.at[unit]
        ).start()

    def attend_temporal():
        def arrived(step, carry):
            peer = tm_peer(step)
            t_copy(peer, peer).wait_recv()
            return carry

        lax.fori_loop(1, TM, arrived, 0)
        width = TM * FR * GROUP
        row = lax.broadcasted_iota(jnp.int32, (width, width), 0)
        column = lax.broadcasted_iota(jnp.int32, (width, width), 1)
        same = (row % GROUP) == (column % GROUP)
        allowed = same & (column < count_ref[0] * GROUP)

        def group(index, carry):
            span = pl.ds(pl.multiple_of(index * GROUP, GROUP), GROUP)
            queries = t_recv[:, 0, :, span].reshape(width, HD)
            keys = t_recv[:, 1, :, span].reshape(width, HD)
            values = t_recv[:, 2, :, span].reshape(width, HD)
            scores = lax.dot_general(queries, keys, CONTRACT_LAST, preferred_element_type=jnp.float32)
            weights, total = softmax_parts(jnp.where(allowed, scores, MASKED))
            mixed = jnp.dot(weights, values, preferred_element_type=jnp.float32)
            t_out[:, :, span] = (mixed / total).astype(jnp.bfloat16).reshape(TM, FR, GROUP, HD)
            return carry

        lax.fori_loop(0, HALF // GROUP, group, 0)

        def back(step, carry):
            t_back_copy(tm_peer(step), tm).start()
            return carry

        lax.fori_loop(1, TM, back, 0)
        pltpu.make_async_copy(
            t_out.at[tm], r_ref.at[SPACE_HEADS + tm // 2, :, pl.ds(HALF * lax.rem(tm, 2), HALF)], t_local_sem
        ).start()

    def temporal_out():
        for index in range(3):
            load_copy(1, index).wait()
        stage_temporal()
        meet_tm()
        send_temporal()

    for place, unit in enumerate(UNIT_ORDER):
        if place == 2:
            temporal_out()
        send_unit(unit)
    for place, unit in enumerate(UNIT_ORDER):
        if place == 1:
            attend_temporal()
        attend_unit(unit)

    def finish_unit(unit, carry):
        def one(step, inner):
            peer = space_peer(step)
            fwd_copy(unit, peer, space).wait_send()
            back_copy(unit, peer, space).wait_send()
            back_copy(unit, peer, peer).wait_recv()
            return inner

        lax.fori_loop(1, SPACE, one, 0)
        pltpu.make_async_copy(
            out_stage.at[unit, space], r_ref.at[2 * space + unit // 2, lax.rem(unit, 2)], local_sem.at[unit]
        ).wait()
        return carry

    lax.fori_loop(0, UNITS, finish_unit, 0)

    def finish_temporal(step, carry):
        peer = tm_peer(step)
        t_copy(peer, tm).wait_send()
        t_back_copy(peer, tm).wait_send()
        t_back_copy(peer, peer).wait_recv()
        return carry

    lax.fori_loop(1, TM, finish_temporal, 0)
    pltpu.make_async_copy(
        t_out.at[tm], r_ref.at[SPACE_HEADS + tm // 2, :, pl.ds(HALF * lax.rem(tm, 2), HALF)], t_local_sem
    ).wait()

    for frame in range(FR):
        present = FR * tm + frame < count_ref[0]
        for head in range(HEADS):
            rows = r_ref[places[head], frame]
            out_ref[frame, :, head * HD:(head + 1) * HD] = jnp.where(present, rows, jnp.zeros_like(rows))


def attend_call(head_class, frame_count, query, key_proj, value):
    block = (ROWS, HD)
    smem = pl.BlockSpec(memory_space=pltpu.SMEM)
    hbm = pl.BlockSpec(memory_space=pltpu.HBM)
    return pl.pallas_call(
        attend_kernel,
        out_shape=pltpu.VMEM((FR, ROWS, HEADS * HD), jnp.bfloat16),
        in_specs=[smem, smem, hbm, hbm, hbm],
        out_specs=pl.BlockSpec(memory_space=pltpu.VMEM),
        scratch_shapes=[
            pltpu.VMEM((HEADS, FR) + block, jnp.bfloat16),
            pltpu.VMEM((3, ROWS, HEADS * HD), jnp.bfloat16),
            pltpu.VMEM((3, ROWS, HEADS * HD), jnp.bfloat16),
            pltpu.SMEM((HEADS,), jnp.int32),
            pltpu.SemaphoreType.DMA((FR, 3)),
            pltpu.VMEM((UNITS, SPACE, 3) + block, jnp.bfloat16),
            pltpu.VMEM((UNITS, SPACE, 3) + block, jnp.bfloat16),
            pltpu.VMEM((TM, 3, FR, HALF, HD), jnp.bfloat16),
            pltpu.VMEM((TM, 3, FR, HALF, HD), jnp.bfloat16),
            pltpu.VMEM((UNITS, SPACE) + block, jnp.bfloat16),
            pltpu.VMEM((TM, FR, HALF, HD), jnp.bfloat16),
            pltpu.SemaphoreType.DMA((UNITS, SPACE)),
            pltpu.SemaphoreType.DMA((UNITS, SPACE)),
            pltpu.SemaphoreType.DMA((TM,)),
            pltpu.SemaphoreType.DMA((TM,)),
            pltpu.SemaphoreType.DMA((UNITS, SPACE)),
            pltpu.SemaphoreType.DMA((UNITS, SPACE)),
            pltpu.SemaphoreType.DMA((TM,)),
            pltpu.SemaphoreType.DMA((TM,)),
            pltpu.SemaphoreType.DMA((UNITS,)),
            pltpu.SemaphoreType.DMA,
            pltpu.SemaphoreType.REGULAR,
            pltpu.SemaphoreType.REGULAR,
        ],
        compiler_params=pltpu.CompilerParams(
            collective_id=0, has_side_effects=True, vmem_limit_bytes=52 * 2**20
        ),
        name="attend",
    )(head_class, frame_count, query, key_proj, value)


def on_device(query, key_proj, value, head_class, frame_count):
    return attend_call(head_class, frame_count, query, key_proj, value)


def solution(mesh):
    return jax.shard_map(
        on_device,
        mesh=mesh,
        in_specs=(P("tm", "space", None), P("tm", "space", None), P("tm", "space", None), P(), P()),
        out_specs=P("tm", "space", None),
        check_vma=False,
    )
```

```python
import functools

import jax
import jax.numpy as jnp
from jax import lax
from jax.experimental import pallas as pl
from jax.experimental.pallas import tpu as pltpu
from jax.sharding import PartitionSpec as P

HEADS = 24
TEMP_HEADS = 8
SPACE_HEADS = HEADS - TEMP_HEADS
HD = 128
FR = 2
ROWS = 256
TM = 16
SPACE = 8
UNITS = 4
HALF = ROWS // 2
GROUP = 16
HUB = SPACE - 1
GATE = SPACE - 2
UNIT_ORDER = (0, 2, 1, 3)
LOG2E = 1.4426950408889634
EXP_SCALE = HD**-0.5 * LOG2E
MASKED = -1e30
MESH = pl.DeviceIdType.MESH
CONTRACT_LAST = (((1,), (1,)), ((), ()))


def softmax_parts(scores):
    peak = jnp.max(scores, axis=-1, keepdims=True)
    weights = jnp.exp2((scores - peak) * EXP_SCALE)
    return weights.astype(jnp.bfloat16), jnp.sum(weights, axis=-1, keepdims=True)


def head_places(class_ref):
    places, spatial, temporal = [], jnp.int32(0), jnp.int32(SPACE_HEADS)
    for head in range(HEADS):
        kind = class_ref[head]
        places.append(jnp.where(kind == 0, spatial, temporal))
        spatial = spatial + (1 - kind)
        temporal = temporal + kind
    return places


def attend_kernel(
    class_ref, count_ref, q_ref, k_ref, v_ref, out_ref,
    r_ref, held_first, held_second, order_ref, load_sem, stage, recv, t_stage, t_recv, out_stage, t_out,
    fwd_send, fwd_recv, t_send, t_recv_sem, back_send, back_recv, tb_send, tb_recv, local_sem, t_local_sem,
    space_go, tm_go,
):
    tm = lax.axis_index("tm")
    space = lax.axis_index("space")
    tensors = (q_ref, k_ref, v_ref)
    held = (held_first, held_second)

    def load_copy(frame, index):
        return pltpu.make_async_copy(tensors[index].at[frame], held[frame].at[index], load_sem.at[frame, index])

    for index in range(3):
        load_copy(0, index).start()

    def space_peer(step):
        return lax.rem(space // 2 + step // 2, 4) * 2 + lax.rem(space + step, 2)

    def tm_peer(step):
        high = lax.rem(tm // 8 + step // 8, 2)
        depth = lax.rem(tm // 2 + step // 2, 4)
        return (high * 4 + depth) * 2 + lax.rem(tm + step, 2)

    def fwd_copy(unit, peer, slot):
        return pltpu.make_async_remote_copy(
            src_ref=stage.at[unit, peer], dst_ref=recv.at[unit, slot],
            send_sem=fwd_send.at[unit, peer], recv_sem=fwd_recv.at[unit, slot],
            device_id=(tm, peer), device_id_type=MESH,
        )

    def back_copy(unit, peer, owner):
        return pltpu.make_async_remote_copy(
            src_ref=out_stage.at[unit, peer],
            dst_ref=r_ref.at[2 * owner + unit // 2, lax.rem(unit, 2)],
            send_sem=back_send.at[unit, peer], recv_sem=back_recv.at[unit, owner],
            device_id=(tm, peer), device_id_type=MESH,
        )

    def t_copy(peer, slot):
        return pltpu.make_async_remote_copy(
            src_ref=t_stage.at[peer], dst_ref=t_recv.at[slot],
            send_sem=t_send.at[peer], recv_sem=t_recv_sem.at[slot],
            device_id=(peer, space), device_id_type=MESH,
        )

    def t_back_copy(peer, owner):
        return pltpu.make_async_remote_copy(
            src_ref=t_out.at[peer],
            dst_ref=r_ref.at[SPACE_HEADS + owner // 2, :, pl.ds(HALF * lax.rem(owner, 2), HALF)],
            send_sem=tb_send.at[peer], recv_sem=tb_recv.at[owner],
            device_id=(peer, space), device_id_type=MESH,
        )

    barrier = pltpu.get_barrier_semaphore()

    def tell_space(sem, me):
        for other in range(SPACE):
            if other != me:
                pl.semaphore_signal(sem, inc=1, device_id=(tm, other), device_id_type=MESH)

    @pl.when(space != HUB)
    def _():
        pl.semaphore_signal(barrier, inc=1, device_id=(tm, HUB), device_id_type=MESH)

    @pl.when(space == HUB)
    def _():
        pl.semaphore_wait(barrier, SPACE - 1)
        tell_space(space_go, HUB)

    def meet_space():
        @pl.when(space != HUB)
        def _():
            pl.semaphore_wait(space_go, 1)

        @pl.when(space == GATE)
        def _():
            def greet(step, carry):
                pl.semaphore_signal(barrier, inc=1, device_id=(tm_peer(step), GATE), device_id_type=MESH)
                return carry

            lax.fori_loop(1, TM, greet, 0)

    def meet_tm():
        @pl.when(space == GATE)
        def _():
            pl.semaphore_wait(barrier, TM - 1)
            tell_space(tm_go, GATE)

        @pl.when(space != GATE)
        def _():
            pl.semaphore_wait(tm_go, 1)

    def send_unit(unit):
        def pick(peer, refs):
            head = order_ref[2 * peer + unit // 2]
            lanes = pl.ds(head * HD, HD)
            for index in range(3):
                refs[index][...] = held[unit % 2][index, :, lanes]

        def one(step, carry):
            peer = space_peer(step)
            pick(peer, [stage.at[unit, peer, index] for index in range(3)])
            fwd_copy(unit, peer, space).start()
            return carry

        lax.fori_loop(1, SPACE, one, 0)
        pick(space, [recv.at[unit, space, index] for index in range(3)])

    def stage_temporal():
        def one(step, carry):
            head = order_ref[SPACE_HEADS + step]
            lanes = pl.ds(head * HD, HD)
            for index in range(3):
                for half in range(2):
                    for frame in range(FR):
                        t_stage[2 * step + half, index, frame] = held[frame][index, half * HALF:(half + 1) * HALF, lanes]
            return carry

        lax.fori_loop(0, TEMP_HEADS, one, 0)

    def send_temporal():
        def one(step, carry):
            t_copy(tm_peer(TM - step), tm).start()
            return carry

        lax.fori_loop(1, TM, one, 0)
        t_recv[tm] = t_stage[tm]

    places = head_places(class_ref)
    for place in range(HEADS):
        order_ref[place] = sum(jnp.where(places[head] == place, head, 0) for head in range(HEADS))
    for index in range(3):
        load_copy(0, index).wait()
    for index in range(3):
        load_copy(1, index).start()
    meet_space()
    def attend_unit(unit):
        def arrived(step, carry):
            peer = space_peer(step)
            fwd_copy(unit, peer, peer).wait_recv()
            return carry

        lax.fori_loop(1, SPACE, arrived, 0)
        present = FR * tm + unit % FR < count_ref[0]

        def block(step, carry):
            peer = space_peer(lax.rem(step + 1, SPACE))
            keys = recv[unit, :, 1].reshape(SPACE * ROWS, HD)
            values = recv[unit, :, 2].reshape(SPACE * ROWS, HD)
            scores = lax.dot_general(
                recv[unit, peer, 0], keys, CONTRACT_LAST, preferred_element_type=jnp.float32
            )
            weights, total = softmax_parts(scores)
            mixed = jnp.dot(weights, values, preferred_element_type=jnp.float32)
            out_stage[unit, peer] = jnp.where(present, mixed / total, 0.0).astype(jnp.bfloat16)

            @pl.when(step < SPACE - 1)
            def _():
                back_copy(unit, peer, space).start()

            return carry

        lax.fori_loop(0, SPACE, block, 0)
        pltpu.make_async_copy(
            out_stage.at[unit, space], r_ref.at[2 * space + unit // 2, lax.rem(unit, 2)], local_sem.at[unit]
        ).start()

    def attend_temporal():
        def arrived(step, carry):
            peer = tm_peer(step)
            t_copy(peer, peer).wait_recv()
            return carry

        lax.fori_loop(1, TM, arrived, 0)
        width = TM * FR * GROUP
        row = lax.broadcasted_iota(jnp.int32, (width, width), 0)
        column = lax.broadcasted_iota(jnp.int32, (width, width), 1)
        same = (row % GROUP) == (column % GROUP)
        allowed = same & (column < count_ref[0] * GROUP)
        present = lax.broadcasted_iota(jnp.int32, (width, HD), 0) < count_ref[0] * GROUP

        def group(index, carry):
            span = pl.ds(pl.multiple_of(index * GROUP, GROUP), GROUP)
            queries = t_recv[:, 0, :, span].reshape(width, HD)
            keys = t_recv[:, 1, :, span].reshape(width, HD)
            values = t_recv[:, 2, :, span].reshape(width, HD)
            scores = lax.dot_general(queries, keys, CONTRACT_LAST, preferred_element_type=jnp.float32)
            weights, total = softmax_parts(jnp.where(allowed, scores, MASKED))
            mixed = jnp.dot(weights, values, preferred_element_type=jnp.float32)
            mixed = jnp.where(present, mixed / total, 0.0)
            t_out[:, :, span] = mixed.astype(jnp.bfloat16).reshape(TM, FR, GROUP, HD)
            return carry

        lax.fori_loop(0, HALF // GROUP, group, 0)

        def back(step, carry):
            t_back_copy(tm_peer(step), tm).start()
            return carry

        lax.fori_loop(1, TM, back, 0)
        pltpu.make_async_copy(
            t_out.at[tm], r_ref.at[SPACE_HEADS + tm // 2, :, pl.ds(HALF * lax.rem(tm, 2), HALF)], t_local_sem
        ).start()

    def temporal_out():
        for index in range(3):
            load_copy(1, index).wait()
        stage_temporal()
        meet_tm()
        send_temporal()

    for place, unit in enumerate(UNIT_ORDER):
        if place == 2:
            temporal_out()
        send_unit(unit)
    for place, unit in enumerate(UNIT_ORDER):
        if place == 1:
            attend_temporal()
        attend_unit(unit)

    def finish_unit(unit, carry):
        def one(step, inner):
            peer = space_peer(step)
            fwd_copy(unit, peer, space).wait_send()
            back_copy(unit, peer, space).wait_send()
            back_copy(unit, peer, peer).wait_recv()
            return inner

        lax.fori_loop(1, SPACE, one, 0)
        pltpu.make_async_copy(
            out_stage.at[unit, space], r_ref.at[2 * space + unit // 2, lax.rem(unit, 2)], local_sem.at[unit]
        ).wait()
        return carry

    lax.fori_loop(0, UNITS, finish_unit, 0)

    def finish_temporal(step, carry):
        peer = tm_peer(step)
        t_copy(peer, tm).wait_send()
        t_back_copy(peer, tm).wait_send()
        t_back_copy(peer, peer).wait_recv()
        return carry

    lax.fori_loop(1, TM, finish_temporal, 0)
    pltpu.make_async_copy(
        t_out.at[tm], r_ref.at[SPACE_HEADS + tm // 2, :, pl.ds(HALF * lax.rem(tm, 2), HALF)], t_local_sem
    ).wait()

    for frame in range(FR):
        for head in range(HEADS):
            out_ref[frame, :, head * HD:(head + 1) * HD] = r_ref[places[head], frame]


def attend_call(head_class, frame_count, query, key_proj, value):
    block = (ROWS, HD)
    smem = pl.BlockSpec(memory_space=pltpu.SMEM)
    hbm = pl.BlockSpec(memory_space=pltpu.HBM)
    return pl.pallas_call(
        attend_kernel,
        out_shape=pltpu.VMEM((FR, ROWS, HEADS * HD), jnp.bfloat16),
        in_specs=[smem, smem, hbm, hbm, hbm],
        out_specs=pl.BlockSpec(memory_space=pltpu.VMEM),
        scratch_shapes=[
            pltpu.VMEM((HEADS, FR) + block, jnp.bfloat16),
            pltpu.VMEM((3, ROWS, HEADS * HD), jnp.bfloat16),
            pltpu.VMEM((3, ROWS, HEADS * HD), jnp.bfloat16),
            pltpu.SMEM((HEADS,), jnp.int32),
            pltpu.SemaphoreType.DMA((FR, 3)),
            pltpu.VMEM((UNITS, SPACE, 3) + block, jnp.bfloat16),
            pltpu.VMEM((UNITS, SPACE, 3) + block, jnp.bfloat16),
            pltpu.VMEM((TM, 3, FR, HALF, HD), jnp.bfloat16),
            pltpu.VMEM((TM, 3, FR, HALF, HD), jnp.bfloat16),
            pltpu.VMEM((UNITS, SPACE) + block, jnp.bfloat16),
            pltpu.VMEM((TM, FR, HALF, HD), jnp.bfloat16),
            pltpu.SemaphoreType.DMA((UNITS, SPACE)),
            pltpu.SemaphoreType.DMA((UNITS, SPACE)),
            pltpu.SemaphoreType.DMA((TM,)),
            pltpu.SemaphoreType.DMA((TM,)),
            pltpu.SemaphoreType.DMA((UNITS, SPACE)),
            pltpu.SemaphoreType.DMA((UNITS, SPACE)),
            pltpu.SemaphoreType.DMA((TM,)),
            pltpu.SemaphoreType.DMA((TM,)),
            pltpu.SemaphoreType.DMA((UNITS,)),
            pltpu.SemaphoreType.DMA,
            pltpu.SemaphoreType.REGULAR,
            pltpu.SemaphoreType.REGULAR,
        ],
        compiler_params=pltpu.CompilerParams(
            collective_id=0, has_side_effects=True, vmem_limit_bytes=52 * 2**20
        ),
        name="attend",
    )(head_class, frame_count, query, key_proj, value)


def on_device(query, key_proj, value, head_class, frame_count):
    return attend_call(head_class, frame_count, query, key_proj, value)


def solution(mesh):
    return jax.shard_map(
        on_device,
        mesh=mesh,
        in_specs=(P("tm", "space", None), P("tm", "space", None), P("tm", "space", None), P(), P()),
        out_specs=P("tm", "space", None),
        check_vma=False,
    )
```

```python
import functools

import jax
import jax.numpy as jnp
from jax import lax
from jax.experimental import pallas as pl
from jax.experimental.pallas import tpu as pltpu
from jax.sharding import PartitionSpec as P

HEADS = 24
TEMP_HEADS = 8
SPACE_HEADS = HEADS - TEMP_HEADS
HD = 128
FR = 2
ROWS = 256
TM = 16
SPACE = 8
UNITS = 4
HALF = ROWS // 2
GROUP = 16
HUB = SPACE - 1
GATE = SPACE - 2
UNIT_ORDER = (0, 2, 1, 3)
LOG2E = 1.4426950408889634
EXP_SCALE = HD**-0.5 * LOG2E
MASKED = -1e30
MESH = pl.DeviceIdType.MESH
CONTRACT_LAST = (((1,), (1,)), ((), ()))


def softmax_parts(scores):
    peak = jnp.max(scores, axis=-1, keepdims=True)
    weights = jnp.exp2((scores - peak) * EXP_SCALE)
    return weights.astype(jnp.bfloat16), jnp.sum(weights, axis=-1, keepdims=True)


def head_places(class_ref):
    places, spatial, temporal = [], jnp.int32(0), jnp.int32(SPACE_HEADS)
    for head in range(HEADS):
        kind = class_ref[head]
        places.append(jnp.where(kind == 0, spatial, temporal))
        spatial = spatial + (1 - kind)
        temporal = temporal + kind
    return places


def attend_kernel(
    class_ref, count_ref, q_ref, k_ref, v_ref, out_ref,
    r_ref, held_first, held_second, order_ref, load_sem, stage, recv, t_stage, t_recv, out_stage, t_out,
    fwd_send, fwd_recv, t_send, t_recv_sem, back_send, back_recv, tb_send, tb_recv, local_sem, t_local_sem,
    space_go, tm_go,
):
    tm = lax.axis_index("tm")
    space = lax.axis_index("space")
    tensors = (q_ref, k_ref, v_ref)
    held = (held_first, held_second)

    def load_copy(frame, index):
        return pltpu.make_async_copy(tensors[index].at[frame], held[frame].at[index], load_sem.at[frame, index])

    for index in range(3):
        load_copy(0, index).start()

    def space_peer(step):
        return lax.rem(space // 2 + step // 2, 4) * 2 + lax.rem(space + step, 2)

    def tm_peer(step):
        high = lax.rem(tm // 8 + step // 8, 2)
        depth = lax.rem(tm // 2 + step // 2, 4)
        return (high * 4 + depth) * 2 + lax.rem(tm + step, 2)

    def fwd_copy(unit, peer, slot):
        return pltpu.make_async_remote_copy(
            src_ref=stage.at[unit, peer], dst_ref=recv.at[unit, slot],
            send_sem=fwd_send.at[unit, peer], recv_sem=fwd_recv.at[unit, slot],
            device_id=(tm, peer), device_id_type=MESH,
        )

    def back_copy(unit, peer, owner):
        return pltpu.make_async_remote_copy(
            src_ref=out_stage.at[unit, peer],
            dst_ref=r_ref.at[2 * owner + unit // 2, lax.rem(unit, 2)],
            send_sem=back_send.at[unit, peer], recv_sem=back_recv.at[unit, owner],
            device_id=(tm, peer), device_id_type=MESH,
        )

    def t_copy(peer, slot):
        return pltpu.make_async_remote_copy(
            src_ref=t_stage.at[peer], dst_ref=t_recv.at[slot],
            send_sem=t_send.at[peer], recv_sem=t_recv_sem.at[slot],
            device_id=(peer, space), device_id_type=MESH,
        )

    def t_back_copy(peer, owner):
        return pltpu.make_async_remote_copy(
            src_ref=t_out.at[peer],
            dst_ref=r_ref.at[SPACE_HEADS + owner // 2, :, pl.ds(HALF * lax.rem(owner, 2), HALF)],
            send_sem=tb_send.at[peer], recv_sem=tb_recv.at[owner],
            device_id=(peer, space), device_id_type=MESH,
        )

    barrier = pltpu.get_barrier_semaphore()

    def tell_space(sem, me):
        for other in range(SPACE):
            if other != me:
                pl.semaphore_signal(sem, inc=1, device_id=(tm, other), device_id_type=MESH)

    @pl.when(space != HUB)
    def _():
        pl.semaphore_signal(barrier, inc=1, device_id=(tm, HUB), device_id_type=MESH)

    @pl.when(space == HUB)
    def _():
        pl.semaphore_wait(barrier, SPACE - 1)
        tell_space(space_go, HUB)

    def meet_space():
        @pl.when(space != HUB)
        def _():
            pl.semaphore_wait(space_go, 1)

        @pl.when(space == GATE)
        def _():
            def greet(step, carry):
                pl.semaphore_signal(barrier, inc=1, device_id=(tm_peer(step), GATE), device_id_type=MESH)
                return carry

            lax.fori_loop(1, TM, greet, 0)

    def meet_tm():
        @pl.when(space == GATE)
        def _():
            pl.semaphore_wait(barrier, TM - 1)
            tell_space(tm_go, GATE)

        @pl.when(space != GATE)
        def _():
            pl.semaphore_wait(tm_go, 1)

    def send_unit(unit):
        def pick(peer, refs):
            head = order_ref[2 * peer + unit // 2]
            lanes = pl.ds(head * HD, HD)
            for index in range(3):
                refs[index][...] = held[unit % 2][index, :, lanes]

        def one(step, carry):
            peer = space_peer(step)
            pick(peer, [stage.at[unit, peer, index] for index in range(3)])
            fwd_copy(unit, peer, space).start()
            return carry

        lax.fori_loop(1, SPACE, one, 0)
        pick(space, [recv.at[unit, space, index] for index in range(3)])

    def stage_temporal():
        def one(step, carry):
            head = order_ref[SPACE_HEADS + step]
            lanes = pl.ds(head * HD, HD)
            for index in range(3):
                for half in range(2):
                    for frame in range(FR):
                        t_stage[2 * step + half, index, frame] = held[frame][index, half * HALF:(half + 1) * HALF, lanes]
            return carry

        lax.fori_loop(0, TEMP_HEADS, one, 0)

    def send_temporal():
        def one(step, carry):
            t_copy(tm_peer(TM - step), tm).start()
            return carry

        lax.fori_loop(1, TM, one, 0)
        t_recv[tm] = t_stage[tm]

    places = head_places(class_ref)
    for place in range(HEADS):
        order_ref[place] = sum(jnp.where(places[head] == place, head, 0) for head in range(HEADS))
    for index in range(3):
        load_copy(0, index).wait()
    for index in range(3):
        load_copy(1, index).start()
    meet_space()
    def attend_unit(unit):
        def arrived(step, carry):
            peer = space_peer(step)
            fwd_copy(unit, peer, peer).wait_recv()
            return carry

        lax.fori_loop(1, SPACE, arrived, 0)
        present = FR * tm + unit % FR < count_ref[0]

        def block(step, carry):
            peer = space_peer(lax.rem(step + 1, SPACE))
            keys = recv[unit, :, 1].reshape(SPACE * ROWS, HD)
            values = recv[unit, :, 2].reshape(SPACE * ROWS, HD)
            scores = lax.dot_general(
                recv[unit, peer, 0], keys, CONTRACT_LAST, preferred_element_type=jnp.float32
            )
            weights, total = softmax_parts(scores)
            mixed = jnp.dot(weights, values, preferred_element_type=jnp.float32)
            out_stage[unit, peer] = jnp.where(present, mixed / total, 0.0).astype(jnp.bfloat16)

            @pl.when(step < SPACE - 1)
            def _():
                back_copy(unit, peer, space).start()

            return carry

        lax.fori_loop(0, SPACE, block, 0)
        pltpu.make_async_copy(
            out_stage.at[unit, space], r_ref.at[2 * space + unit // 2, lax.rem(unit, 2)], local_sem.at[unit]
        ).start()

    def attend_temporal():
        def arrived(step, carry):
            peer = tm_peer(step)
            t_copy(peer, peer).wait_recv()
            return carry

        lax.fori_loop(1, TM, arrived, 0)
        width = TM * FR * GROUP
        row = lax.broadcasted_iota(jnp.int32, (width, width), 0)
        column = lax.broadcasted_iota(jnp.int32, (width, width), 1)
        same = (row % GROUP) == (column % GROUP)
        allowed = same & (column < count_ref[0] * GROUP)
        present = lax.broadcasted_iota(jnp.int32, (width, HD), 0) < count_ref[0] * GROUP

        def group(index, carry):
            span = pl.ds(pl.multiple_of(index * GROUP, GROUP), GROUP)
            queries = t_recv[:, 0, :, span].reshape(width, HD)
            keys = t_recv[:, 1, :, span].reshape(width, HD)
            values = t_recv[:, 2, :, span].reshape(width, HD)
            scores = lax.dot_general(queries, keys, CONTRACT_LAST, preferred_element_type=jnp.float32)
            weights, total = softmax_parts(jnp.where(allowed, scores, MASKED))
            mixed = jnp.dot(weights, values, preferred_element_type=jnp.float32)
            mixed = jnp.where(present, mixed / total, 0.0)
            t_out[:, :, span] = mixed.astype(jnp.bfloat16).reshape(TM, FR, GROUP, HD)
            return carry

        lax.fori_loop(0, HALF // GROUP, group, 0)

        def back(step, carry):
            t_back_copy(tm_peer(step), tm).start()
            return carry

        lax.fori_loop(1, TM, back, 0)
        pltpu.make_async_copy(
            t_out.at[tm], r_ref.at[SPACE_HEADS + tm // 2, :, pl.ds(HALF * lax.rem(tm, 2), HALF)], t_local_sem
        ).start()

    def temporal_out():
        for index in range(3):
            load_copy(1, index).wait()
        stage_temporal()
        meet_tm()
        send_temporal()

    for place, unit in enumerate(UNIT_ORDER):
        if place == 2:
            temporal_out()
        send_unit(unit)
    for place, unit in enumerate(UNIT_ORDER):
        if place == 1:
            attend_temporal()
        attend_unit(unit)

    def finish_unit(unit, carry):
        def one(step, inner):
            peer = space_peer(step)
            back_copy(unit, peer, peer).wait_recv()
            return inner

        lax.fori_loop(1, SPACE, one, 0)
        pltpu.make_async_copy(
            out_stage.at[unit, space], r_ref.at[2 * space + unit // 2, lax.rem(unit, 2)], local_sem.at[unit]
        ).wait()
        return carry

    lax.fori_loop(0, UNITS, finish_unit, 0)

    def finish_temporal(step, carry):
        peer = tm_peer(step)
        t_back_copy(peer, peer).wait_recv()
        return carry

    lax.fori_loop(1, TM, finish_temporal, 0)
    pltpu.make_async_copy(
        t_out.at[tm], r_ref.at[SPACE_HEADS + tm // 2, :, pl.ds(HALF * lax.rem(tm, 2), HALF)], t_local_sem
    ).wait()

    for frame in range(FR):
        for head in range(HEADS):
            out_ref[frame, :, head * HD:(head + 1) * HD] = r_ref[places[head], frame]

    def units_sent(step, carry):
        peer = space_peer(step)
        for unit in range(UNITS):
            fwd_copy(unit, peer, space).wait_send()
            back_copy(unit, peer, space).wait_send()
        return carry

    def temporal_sent(step, carry):
        peer = tm_peer(step)
        t_copy(peer, tm).wait_send()
        t_back_copy(peer, tm).wait_send()
        return carry

    lax.fori_loop(1, SPACE, units_sent, 0)
    lax.fori_loop(1, TM, temporal_sent, 0)


def attend_call(head_class, frame_count, query, key_proj, value):
    block = (ROWS, HD)
    smem = pl.BlockSpec(memory_space=pltpu.SMEM)
    hbm = pl.BlockSpec(memory_space=pltpu.HBM)
    return pl.pallas_call(
        attend_kernel,
        out_shape=pltpu.VMEM((FR, ROWS, HEADS * HD), jnp.bfloat16),
        in_specs=[smem, smem, hbm, hbm, hbm],
        out_specs=pl.BlockSpec(memory_space=pltpu.VMEM),
        scratch_shapes=[
            pltpu.VMEM((HEADS, FR) + block, jnp.bfloat16),
            pltpu.VMEM((3, ROWS, HEADS * HD), jnp.bfloat16),
            pltpu.VMEM((3, ROWS, HEADS * HD), jnp.bfloat16),
            pltpu.SMEM((HEADS,), jnp.int32),
            pltpu.SemaphoreType.DMA((FR, 3)),
            pltpu.VMEM((UNITS, SPACE, 3) + block, jnp.bfloat16),
            pltpu.VMEM((UNITS, SPACE, 3) + block, jnp.bfloat16),
            pltpu.VMEM((TM, 3, FR, HALF, HD), jnp.bfloat16),
            pltpu.VMEM((TM, 3, FR, HALF, HD), jnp.bfloat16),
            pltpu.VMEM((UNITS, SPACE) + block, jnp.bfloat16),
            pltpu.VMEM((TM, FR, HALF, HD), jnp.bfloat16),
            pltpu.SemaphoreType.DMA((UNITS, SPACE)),
            pltpu.SemaphoreType.DMA((UNITS, SPACE)),
            pltpu.SemaphoreType.DMA((TM,)),
            pltpu.SemaphoreType.DMA((TM,)),
            pltpu.SemaphoreType.DMA((UNITS, SPACE)),
            pltpu.SemaphoreType.DMA((UNITS, SPACE)),
            pltpu.SemaphoreType.DMA((TM,)),
            pltpu.SemaphoreType.DMA((TM,)),
            pltpu.SemaphoreType.DMA((UNITS,)),
            pltpu.SemaphoreType.DMA,
            pltpu.SemaphoreType.REGULAR,
            pltpu.SemaphoreType.REGULAR,
        ],
        compiler_params=pltpu.CompilerParams(
            collective_id=0, has_side_effects=True, vmem_limit_bytes=52 * 2**20
        ),
        name="attend",
    )(head_class, frame_count, query, key_proj, value)


def on_device(query, key_proj, value, head_class, frame_count):
    return attend_call(head_class, frame_count, query, key_proj, value)


def solution(mesh):
    return jax.shard_map(
        on_device,
        mesh=mesh,
        in_specs=(P("tm", "space", None), P("tm", "space", None), P("tm", "space", None), P(), P()),
        out_specs=P("tm", "space", None),
        check_vma=False,
    )
```
